32 devices in a mesh: groups: 2 (over x), row: 8 (over z, y), col: 2 (over core).
Axes of the slice: x: 2, y: 2, z: 4, core: 2. Of those that a mesh axis runs over, the one named last changes fastest.
Arguments:
- counts: int32 [2, 8192, 2048], P(None, ('groups', 'row'), 'col'), parts along dimension 1, may hold values from 0 to 255
- row_factors: float32 [8192, 512], P(('groups', 'row', 'col')), parts along dimension 0, may hold values from -1.5 to 1.5
- row_moments: float32 [8192, 512], P(('groups', 'row', 'col')), parts along dimension 0, may hold values from 64 to 32768
- row_bias: float32 [8192], P(('groups', 'row', 'col')), parts along dimension 0, may hold values from -3 to 3
- row_bias_moments: float32 [8192], P(('groups', 'row', 'col')), parts along dimension 0, may hold values from 262144 to 268435456
- col_factors: float32 [32768, 512], P(('groups', 'row', 'col')), parts along dimension 0, may hold values from -1.5 to 1.5
- col_moments: float32 [32768, 512], P(('groups', 'row', 'col')), parts along dimension 0, may hold values from 16 to 8192
- col_bias: float32 [32768], P(('groups', 'row', 'col')), parts along dimension 0, may hold values from -3 to 3
- col_bias_moments: float32 [32768], P(('groups', 'row', 'col')), parts along dimension 0, may hold values from 16384 to 16777216
Outputs:
- row_factors_out: float32 [8192, 512], P(('groups', 'row', 'col')), parts along dimension 0
- row_bias_out: float32 [8192], P(('groups', 'row', 'col')), parts along dimension 0
- col_factors_out: float32 [32768, 512], P(('groups', 'row', 'col')), parts along dimension 0
- col_bias_out: float32 [32768], P(('groups', 'row', 'col')), parts along dimension 0
The draws below stay inside these ranges and needn't reach their ends.
There are 2 independent parts, one for each index of `groups`. The reference program is written for one: setup_inputs(seed, part) draws one part's arguments, and reference() takes and returns one part's arrays. A program takes and returns all parts, laid end to end along the dimension named above; each array names one. Nothing has to cross between parts.
All inputs are finite; a program needn't handle non-finite values.
Results may differ from the reference program's by a relative error of at most 0.0066.
Values may be sent and summed in bfloat16 or wider, within the bound.
A program may use at most 64 MiB of HBM per device.

```python
import math
import jax
import jax.numpy as jnp
from jax import lax

K = 512
ROWS_DEV = 512
COLS_DEV = 1024
ROUNDS = 2
ROW_BLOCKS = 8
COL_SPLIT = 2
ROWS = 4096
COLS = 16384
TILE_COLS = 2048


def draw_counts(key, part):
    base = jax.random.randint(key, (ROUNDS, ROWS, TILE_COLS), -96, 256)
    clipped = jnp.clip(base, 0, 255)
    return clipped.at[:, 0, 0].set(255).at[:, 0, 1].set(0)


def steps_of(key, dims, pieces, smallest, top_value):
    level = 1.0
    for dim, blocks in pieces:
        draws = jax.random.uniform(jax.random.fold_in(jax.random.fold_in(key, 6), dim), (blocks,), jnp.float32, smallest / len(pieces), top_value / len(pieces))
        level = level * jnp.repeat(jnp.exp(draws), dims[dim] // blocks).reshape((-1,) + (1,) * (len(dims) - 1 - dim))
    return level


def normal_values(own_key, dims, deviation, reach, split=(), dtype=jnp.bfloat16):
    values = jax.random.normal(own_key, dims, jnp.float32) * deviation
    if len(split) > 0:
        values = steps_of(own_key, dims, split, -0.22, 0.18) * values
    return jnp.clip(values, min=-reach, max=reach).astype(dtype)


def setup_inputs(seed: int = 0, part: int = 0) -> dict:
    arg_keys = jax.random.split(jax.random.key(seed), 10)
    part_splits = jax.random.split(jax.random.fold_in(arg_keys[9], part), 10)
    return {
        "counts": draw_counts(jax.random.fold_in(jax.random.fold_in(arg_keys[9], part), 71), part),
        "row_factors": normal_values(part_splits[1], (ROWS, K), 0.25, 1.5, ((0, 16),), jnp.float32),
        "row_moments": jnp.clip(jnp.exp(math.log(32768.0) - 6.2383246 * jax.random.uniform(part_splits[2], (ROWS, K), jnp.float32) ** steps_of(part_splits[2], (ROWS, K), ((0, 16),), -0.2, 0.2)), 64.0, 32768.0),
        "row_bias": normal_values(part_splits[3], (ROWS,), 0.5, 3.0, ((0, 16),), jnp.float32),
        "row_bias_moments": jnp.clip(jnp.exp(math.log(268435456) - 6.931472 * jax.random.uniform(part_splits[4], (ROWS,), jnp.float32) ** steps_of(part_splits[4], (ROWS,), ((0, 16),), -0.2, 0.2)), 262144.0, 268435456),
        "col_factors": normal_values(part_splits[5], (COLS, K), 0.25, 1.5, ((0, 16),), jnp.float32),
        "col_moments": jnp.clip(jnp.exp(math.log(8192.0) - 6.2383246 * jax.random.uniform(part_splits[6], (COLS, K), jnp.float32) ** steps_of(part_splits[6], (COLS, K), ((0, 16),), -0.2, 0.2)), 16.0, 8192.0),
        "col_bias": normal_values(part_splits[7], (COLS,), 0.5, 3.0, ((0, 16),), jnp.float32),
        "col_bias_moments": jnp.clip(jnp.exp(math.log(16777216) - 6.931472 * jax.random.uniform(part_splits[8], (COLS,), jnp.float32) ** steps_of(part_splits[8], (COLS,), ((0, 16),), -0.2, 0.2)), 16384.0, 16777216),
    }


LEARN_RATE = 0.25
COUNT_SCALE = 100.0
WEIGHT_POWER = 0.75

def weights_logs(counts):
    values = counts.astype(jnp.float32)
    weight = jnp.minimum((values / COUNT_SCALE) ** WEIGHT_POWER, 1.0)
    log_count = jnp.log(jnp.maximum(values, 1.0))
    return (weight, log_count)

def adagrad(current, moment, gradient):
    moment = moment + gradient * gradient
    return (current - LEARN_RATE * gradient / jnp.sqrt(moment), moment)

def low_copy(matrix):
    return lax.optimization_barrier(matrix.astype(jnp.bfloat16)).astype(jnp.float32)

def reference(counts, row_factors, row_moments, row_bias, row_bias_moments, col_factors, col_moments, col_bias, col_bias_moments):
    blocks = ROW_BLOCKS
    splits = COL_SPLIT
    row_value = row_factors.reshape(blocks, ROWS_DEV, K)
    row_moment = row_moments.reshape(blocks, ROWS_DEV, K)
    row_level = row_bias.reshape(blocks, ROWS_DEV)
    row_level_mom = row_bias_moments.reshape(blocks, ROWS_DEV)
    col_value = col_factors.reshape(blocks, splits, COLS_DEV, K)
    col_moment = col_moments.reshape(blocks, splits, COLS_DEV, K)
    col_level = col_bias.reshape(blocks, splits, COLS_DEV)
    col_level_mom = col_bias_moments.reshape(blocks, splits, COLS_DEV)
    for number in range(ROUNDS):
        weight, log_count = weights_logs(counts[number].reshape(blocks, ROWS_DEV, splits, COLS_DEV))
        met_value = jnp.roll(col_value, -number, axis=0)
        met_moment = jnp.roll(col_moment, -number, axis=0)
        met_level = jnp.roll(col_level, -number, axis=0)
        met_level_mom = jnp.roll(col_level_mom, -number, axis=0)
        row_low = low_copy(row_value)
        col_low = low_copy(met_value)
        predicted = jnp.einsum('rik,rcjk->ricj', row_low, col_low, precision=lax.Precision.HIGHEST)
        predicted = predicted + row_level[:, :, None, None] + met_level[:, None, :, :]
        residue = weight * (predicted - log_count)
        residue_low = low_copy(residue)
        grad_rows = jnp.einsum('ricj,rcjk->rik', residue_low, col_low, precision=lax.Precision.HIGHEST)
        grad_row_level = lax.optimization_barrier(jnp.sum(residue, axis=(2, 3)))
        grad_cols = jnp.einsum('ricj,rik->rcjk', residue_low, row_low, precision=lax.Precision.HIGHEST)
        grad_col_level = lax.optimization_barrier(jnp.sum(residue, axis=1))
        row_value, row_moment = adagrad(row_value, row_moment, grad_rows)
        row_level, row_level_mom = adagrad(row_level, row_level_mom, grad_row_level)
        met_value, met_moment = adagrad(met_value, met_moment, grad_cols)
        met_level, met_level_mom = adagrad(met_level, met_level_mom, grad_col_level)
        col_value = jnp.roll(met_value, number, axis=0)
        col_moment = jnp.roll(met_moment, number, axis=0)
        col_level = jnp.roll(met_level, number, axis=0)
        col_level_mom = jnp.roll(met_level_mom, number, axis=0)
    return (row_value.reshape(ROWS, K), row_level.reshape(ROWS), col_value.reshape(COLS, K), col_level.reshape(COLS))
```

```python
import functools
import math

import jax
import jax.numpy as jnp
from jax import lax
from jax.experimental import pallas as pl
from jax.experimental.pallas import tpu as pltpu
from jax.sharding import PartitionSpec as P


LEARN_RATE = 0.25
COUNT_SCALE = 100.0
WEIGHT_POWER = 0.75
CHUNKS = 4
EARLY = 2
SUB = 16
LANES = 128
MESH = pl.DeviceIdType.MESH
F32 = jnp.float32
BF16 = jnp.bfloat16


def step(value, moment, grad):
    moment = moment + grad * grad
    return value - LEARN_RATE * grad * lax.rsqrt(moment), moment


def to_column(line):
    return jnp.transpose(jnp.broadcast_to(line, (LANES, line.shape[1])))


def to_line(column):
    return jnp.sum(jnp.transpose(column), axis=0, keepdims=True)


def kernel(
    ring,
    counts, row_factors, row_moments, row_bias, row_bias_mom,
    col_factors, col_moments, col_bias, col_bias_mom,
    row_out, row_bias_out, col_out, col_bias_out,
    c0, c1, vrow, vrmom, vcol, vcmom, col_low,
    rows0, rb0, rows1, rb1, rsend, rbsend, snd, rcv,
    pred, res, rbc, bacc, gro, gin, gob, gib, gc, gcb,
    rbm, cbias, cbm,
    xs, xr, bs, br, xsb, xrb, bsb, brb,
    lsem, osem, ssem, rsem, csem, ksem, xsem, ysem,
    bsem, dsem,
):
    me = lax.axis_index("row")
    mine = lax.axis_index("col")
    other = 1 - mine
    right = lax.rem(me + 1, ring)
    left = lax.rem(me + ring - 1, ring)
    half = vrow.shape[0]
    part = half // CHUNKS
    cols = vcol.shape[0]

    def local(src, dst, k):
        cp = pltpu.make_async_copy(src, dst, lsem.at[k])
        cp.start()
        return cp

    def remote(src, dst, s, r, **where):
        return pltpu.make_async_remote_copy(
            src_ref=src, dst_ref=dst, send_sem=s, recv_sem=r,
            device_id=where, device_id_type=MESH,
        )

    in_row = local(row_factors, vrow, 0)
    in_c1 = [
        local(counts.at[1, :, pl.ds(j * part, part), :], c1.at[j], 1 + j)
        for j in range(CHUNKS)
    ]
    in_col = local(col_factors, vcol, 1 + CHUNKS)
    in_c0 = local(counts.at[0], c0, 2 + CHUNKS)
    in_rmom = local(row_moments, vrmom, 3 + CHUNKS)
    in_cmom = local(col_moments, vcmom, 4 + CHUNKS)

    barrier = pltpu.get_barrier_semaphore()
    pl.semaphore_signal(barrier, inc=1, device_id={"row": left}, device_id_type=MESH)
    pl.semaphore_signal(barrier, inc=1, device_id={"row": right}, device_id_type=MESH)
    pl.semaphore_signal(barrier, inc=1, device_id={"col": other}, device_id_type=MESH)

    in_row.wait()
    rows0[mine] = vrow[...].astype(BF16)
    rb0[mine] = row_bias[...]
    pl.semaphore_wait(barrier, 3)
    swap_rows = remote(rows0.at[mine], rows0.at[mine], ssem.at[0], rsem.at[0], col=other)
    swap_rows.start()
    swap_rb = remote(rb0.at[mine], rb0.at[mine], ssem.at[1], rsem.at[1], col=other)
    swap_rb.start()

    send_counts = [
        remote(snd.at[j], rcv.at[j], csem.at[j], ksem.at[j], row=right)
        for j in range(CHUNKS)
    ]

    def push(j):
        in_c1[j].wait()
        for s in (0, 1):
            snd[j, pl.ds(s * part, part)] = c1[j, s].astype(F32).astype(BF16)
        send_counts[j].start()

    for j in range(EARLY):
        push(j)

    in_col.wait()
    col_low[...] = vcol[...].astype(BF16)
    cbias[...] = col_bias[...]
    cbm[...] = col_bias_mom[...]
    rbm[...] = row_bias_mom[...]
    gc[...] = jnp.zeros_like(gc)
    gcb[...] = jnp.zeros_like(gcb)

    def tile(rows, column_bias, load, store_sum):
        count = rows.shape[0]
        rbc[0:count] = column_bias
        pred[0:count] = lax.dot_general(
            rows, col_low[...], (((1,), (1,)), ((), ())), preferred_element_type=F32
        )

        def body(s, carry):
            o = pl.multiple_of(s * SUB, SUB)
            x = load(o)
            logs = jnp.log(jnp.maximum(x, 1.0))
            weight = jnp.exp(WEIGHT_POWER * (logs - math.log(COUNT_SCALE)))
            weight = jnp.where(x >= 1.0, jnp.minimum(weight, 1.0), 0.0)
            bias = rbc[pl.ds(o, SUB)][:, 0:1]
            value = weight * (pred[pl.ds(o, SUB)] + bias + cbias[...] - logs)
            res[pl.ds(o, SUB)] = value.astype(BF16)
            total = value[:, 0:LANES]
            for k in range(1, cols // LANES):
                total = total + value[:, k * LANES:(k + 1) * LANES]
            rbc[pl.ds(o, SUB)] = total
            down = value[0:8]
            for k in range(1, SUB // 8):
                down = down + value[k * 8:(k + 1) * 8]
            gcb[...] += down
            return carry

        lax.fori_loop(0, count // SUB, body, 0)
        store_sum(rbc[0:count])
        low = res[0:count]
        grad_rows = jnp.dot(low, col_low[...], preferred_element_type=F32)
        gc[...] += lax.dot_general(
            low, rows, (((0,), (0,)), ((), ())), preferred_element_type=F32
        )
        return grad_rows

    def half_tile(which):
        def load(o):
            return c0[which, pl.ds(o, SUB)].astype(F32)

        def store_sum(total):
            gob[which] = to_line(total)

        gro[which] = tile(rows0[which], to_column(rb0[which]), load, store_sum)

    swap_rows.wait()
    swap_rb.wait()
    in_c0.wait()
    half_tile(other)
    swap_gr = remote(gro.at[other], gin, ssem.at[2], rsem.at[2], col=other)
    swap_gr.start()
    swap_gb = remote(gob.at[other], gib, ssem.at[3], rsem.at[3], col=other)
    swap_gb.start()
    half_tile(mine)
    in_rmom.wait()
    swap_gr.wait()
    swap_gb.wait()
    value, moment = step(vrow[...], vrmom[...], gro[mine] + gin[...])
    vrow[...] = value
    vrmom[...] = moment
    rsend[...] = value.astype(BF16)
    value, moment = step(rb0[mine], rbm[...], gob[mine] + gib[...])
    rbsend[...] = value
    rbm[...] = moment
    go_rows = remote(rsend, rows1.at[mine], ssem.at[4], rsem.at[4], row=right)
    go_rows.start()
    go_rb = remote(rbsend, rb1.at[mine], ssem.at[5], rsem.at[5], row=right)
    go_rb.start()
    for j in range(EARLY, CHUNKS):
        push(j)

    def col_step():
        def body(s, carry):
            at = pl.ds(pl.multiple_of(s * 64, 64), 64)
            value, moment = step(vcol[at], vcmom[at], gc[at])
            vcol[at] = value
            vcmom[at] = moment
            col_low[at] = value.astype(BF16)
            return carry

        lax.fori_loop(0, cols // 64, body, 0)
        grad = jnp.sum(gcb[...], axis=0, keepdims=True)
        value, moment = step(cbias[...], cbm[...], grad)
        cbias[...] = value
        cbm[...] = moment

    in_cmom.wait()
    col_step()
    gc[...] = jnp.zeros_like(gc)
    gcb[...] = jnp.zeros_like(gcb)

    go_rows.wait()
    pass_rows = remote(rows1.at[mine], rows1.at[mine], ssem.at[6], rsem.at[6], col=other)
    pass_rows.start()
    go_rb.wait()
    pass_rb = remote(rb1.at[mine], rb1.at[mine], ssem.at[7], rsem.at[7], col=other)
    pass_rb.start()
    pass_rows.wait()
    pass_rb.wait()

    swaps = [
        remote(xs.at[j, other], xr.at[j], xsem.at[j], ysem.at[j], col=other)
        for j in range(CHUNKS)
    ]
    backs = [
        remote(bs.at[j], br.at[j], bsem.at[j], dsem.at[j], row=left)
        for j in range(CHUNKS)
    ]

    def give_back(j):
        swaps[j].wait()
        bs[j] = (xs[j, mine] + xr[j]).astype(BF16)
        backs[j].start()

    rbcol = [to_column(rb1[s]) for s in (0, 1)]
    for j in range(CHUNKS):
        send_counts[j].wait()
        at = slice(j * part, (j + 1) * part)

        def load(o):
            return rcv[j, pl.ds(o, SUB)].astype(F32)

        def store_sum(total):
            for s in (0, 1):
                bacc[s, at] = total[s * part:(s + 1) * part]

        rows = jnp.concatenate([rows1[0, at], rows1[1, at]], axis=0)
        bias = jnp.concatenate([rbcol[0][at], rbcol[1][at]], axis=0)
        grad = tile(rows, bias, load, store_sum)
        for s in (0, 1):
            xs[j, s] = grad[s * part:(s + 1) * part]
        swaps[j].start()
        if j > 0:
            give_back(j - 1)

    for s in (0, 1):
        xsb[s] = to_line(bacc[s])
    swap_b = remote(xsb.at[other], xrb, ssem.at[8], rsem.at[8], col=other)
    swap_b.start()
    give_back(CHUNKS - 1)
    swap_b.wait()
    bsb[...] = xsb[mine] + xrb[...]
    back_b = remote(bsb, brb, ssem.at[9], rsem.at[9], row=left)
    back_b.start()

    col_step()
    out_col = pltpu.make_async_copy(vcol, col_out, osem.at[0])
    out_col.start()
    col_bias_out[...] = cbias[...]

    for j in range(CHUNKS):
        backs[j].wait()
        at = slice(j * part, (j + 1) * part)
        value, moment = step(vrow[at], vrmom[at], br[j].astype(F32))
        vrow[at] = value
    out_row = pltpu.make_async_copy(vrow, row_out, osem.at[1])
    out_row.start()
    back_b.wait()
    value, moment = step(rbsend[...], rbm[...], brb[...])
    row_bias_out[...] = value
    out_col.wait()
    out_row.wait()


def per_device(
    ring,
    counts,
    row_factors,
    row_moments,
    row_bias,
    row_bias_moments,
    col_factors,
    col_moments,
    col_bias,
    col_bias_moments,
):
    rounds, height, cols = counts.shape
    half, rank = row_factors.shape
    part = half // CHUNKS
    hbm = pl.BlockSpec(memory_space=pl.ANY)
    vmem = pl.BlockSpec(memory_space=pltpu.VMEM)
    dma = pltpu.SemaphoreType.DMA
    scratch = [
        pltpu.VMEM((2, half, cols), jnp.int32),
        pltpu.VMEM((CHUNKS, 2, part, cols), jnp.int32),
        pltpu.VMEM((half, rank), F32),
        pltpu.VMEM((half, rank), F32),
        pltpu.VMEM((cols, rank), F32),
        pltpu.VMEM((cols, rank), F32),
        pltpu.VMEM((cols, rank), BF16),
        pltpu.VMEM((2, half, rank), BF16),
        pltpu.VMEM((2, 1, half), F32),
        pltpu.VMEM((2, half, rank), BF16),
        pltpu.VMEM((2, 1, half), F32),
        pltpu.VMEM((half, rank), BF16),
        pltpu.VMEM((1, half), F32),
        pltpu.VMEM((CHUNKS, 2 * part, cols), BF16),
        pltpu.VMEM((CHUNKS, 2 * part, cols), BF16),
        pltpu.VMEM((half, cols), F32),
        pltpu.VMEM((half, cols), BF16),
        pltpu.VMEM((half, LANES), F32),
        pltpu.VMEM((2, half, LANES), F32),
        pltpu.VMEM((2, half, rank), F32),
        pltpu.VMEM((half, rank), F32),
        pltpu.VMEM((2, 1, half), F32),
        pltpu.VMEM((1, half), F32),
        pltpu.VMEM((cols, rank), F32),
        pltpu.VMEM((8, cols), F32),
        pltpu.VMEM((1, half), F32),
        pltpu.VMEM((1, cols), F32),
        pltpu.VMEM((1, cols), F32),
        pltpu.VMEM((CHUNKS, 2, part, rank), F32),
        pltpu.VMEM((CHUNKS, part, rank), F32),
        pltpu.VMEM((CHUNKS, part, rank), BF16),
        pltpu.VMEM((CHUNKS, part, rank), BF16),
        pltpu.VMEM((2, 1, half), F32),
        pltpu.VMEM((1, half), F32),
        pltpu.VMEM((1, half), F32),
        pltpu.VMEM((1, half), F32),
        dma((5 + CHUNKS,)),
        dma((2,)),
        dma((10,)),
        dma((10,)),
        dma((CHUNKS,)),
        dma((CHUNKS,)),
        dma((CHUNKS,)),
        dma((CHUNKS,)),
        dma((CHUNKS,)),
        dma((CHUNKS,)),
    ]
    row_new, row_level, col_new, col_level = pl.pallas_call(
        functools.partial(kernel, ring),
        out_shape=(
            jax.ShapeDtypeStruct((half, rank), F32),
            jax.ShapeDtypeStruct((1, half), F32),
            jax.ShapeDtypeStruct((cols, rank), F32),
            jax.ShapeDtypeStruct((1, cols), F32),
        ),
        in_specs=[hbm, hbm, hbm, vmem, vmem, hbm, hbm, vmem, vmem],
        out_specs=(hbm, vmem, hbm, vmem),
        scratch_shapes=scratch,
        compiler_params=pltpu.CompilerParams(
            collective_id=0, has_side_effects=True, vmem_limit_bytes=48 * 1024 * 1024
        ),
    )(
        counts.reshape(rounds, 2, half, cols),
        row_factors,
        row_moments,
        row_bias.reshape(1, half),
        row_bias_moments.reshape(1, half),
        col_factors,
        col_moments,
        col_bias.reshape(1, cols),
        col_bias_moments.reshape(1, cols),
    )
    return row_new, row_level.reshape(half), col_new, col_level.reshape(cols)


def solution(mesh):
    in_specs = (
        P(None, ("groups", "row"), "col"),
        P(("groups", "row", "col"), None),
        P(("groups", "row", "col"), None),
        P(("groups", "row", "col")),
        P(("groups", "row", "col")),
        P(("groups", "row", "col"), None),
        P(("groups", "row", "col"), None),
        P(("groups", "row", "col")),
        P(("groups", "row", "col")),
    )
    out_specs = (
        P(("groups", "row", "col"), None),
        P(("groups", "row", "col")),
        P(("groups", "row", "col"), None),
        P(("groups", "row", "col")),
    )
    return jax.shard_map(
        functools.partial(per_device, mesh.shape["row"]),
        mesh=mesh, in_specs=in_specs, out_specs=out_specs, check_vma=False,
    )
```

```python
import functools
import math

import jax
import jax.numpy as jnp
from jax import lax
from jax.experimental import pallas as pl
from jax.experimental.pallas import tpu as pltpu
from jax.sharding import PartitionSpec as P


LEARN_RATE = 0.25
COUNT_SCALE = 100.0
WEIGHT_POWER = 0.75
CHUNKS = 4
EARLY = 3
SUB = 16
UNROLL = 4
BEFORE = 2
LANES = 128
MESH = pl.DeviceIdType.MESH
F32 = jnp.float32
BF16 = jnp.bfloat16


def step(value, moment, grad):
    moment = moment + grad * grad
    return value - LEARN_RATE * grad * lax.rsqrt(moment), moment


def to_column(line):
    return jnp.transpose(jnp.broadcast_to(line, (LANES, line.shape[1])))


def to_line(column):
    return jnp.sum(jnp.transpose(column), axis=0, keepdims=True)


def kernel(
    ring,
    counts, row_factors, row_moments, row_bias, row_bias_mom,
    col_factors, col_moments, col_bias, col_bias_mom,
    row_out, row_bias_out, col_out, col_bias_out,
    c0, c1, vrow, vrmom, vcol, vcmom, col_low,
    rows0, rb0, rows1, rb1, rsend, rbsend, snd, rcv,
    pred, res, rbc, bacc, gro, gin, gob, gib, gc, gcb,
    rbm, cbias, cbm, wgt, lgs,
    xs, xr, bs, br, xsb, xrb, bsb, brb,
    lsem, ssem, rsem, csem, ksem, xsem, ysem,
    bsem, dsem,
):
    me = lax.axis_index("row")
    mine = lax.axis_index("col")
    other = 1 - mine
    right = lax.rem(me + 1, ring)
    left = lax.rem(me + ring - 1, ring)
    half = vrow.shape[0]
    part = half // CHUNKS
    cols = vcol.shape[0]

    def local(src, dst, k):
        cp = pltpu.make_async_copy(src, dst, lsem.at[k])
        cp.start()
        return cp

    def remote(src, dst, s, r, **where):
        return pltpu.make_async_remote_copy(
            src_ref=src, dst_ref=dst, send_sem=s, recv_sem=r,
            device_id=where, device_id_type=MESH,
        )

    in_row = local(row_factors, vrow, 0)
    in_rb = local(row_bias, rb0.at[mine], 5 + CHUNKS)
    in_c1 = [
        local(counts.at[1, :, pl.ds(j * part, part), :], c1.at[j], 1 + j)
        for j in range(CHUNKS)
    ]
    in_col = local(col_factors, vcol, 1 + CHUNKS)
    in_c0 = local(counts.at[0], c0, 2 + CHUNKS)
    in_rmom = local(row_moments, vrmom, 3 + CHUNKS)
    in_cmom = local(col_moments, vcmom, 4 + CHUNKS)

    in_small = [
        local(row_bias_mom, rbm, 6 + CHUNKS),
        local(col_bias, cbias, 7 + CHUNKS),
        local(col_bias_mom, cbm, 8 + CHUNKS),
    ]

    barrier = pltpu.get_barrier_semaphore()
    pl.semaphore_signal(barrier, inc=1, device_id={"row": left}, device_id_type=MESH)
    pl.semaphore_signal(barrier, inc=1, device_id={"row": right}, device_id_type=MESH)
    pl.semaphore_signal(barrier, inc=1, device_id={"col": other}, device_id_type=MESH)

    in_row.wait()
    rows0[mine] = vrow[...].astype(BF16)
    in_rb.wait()
    pl.semaphore_wait(barrier, 3)
    swap_rows = remote(rows0.at[mine], rows0.at[mine], ssem.at[0], rsem.at[0], col=other)
    swap_rows.start()
    swap_rb = remote(rb0.at[mine], rb0.at[mine], ssem.at[1], rsem.at[1], col=other)
    swap_rb.start()

    send_counts = [
        remote(snd.at[j], rcv.at[j], csem.at[j], ksem.at[j], row=right)
        for j in range(CHUNKS)
    ]

    def push(j):
        in_c1[j].wait()
        for s in (0, 1):
            snd[j, pl.ds(s * part, part)] = c1[j, s].astype(F32).astype(BF16)
        send_counts[j].start()

    for j in range(EARLY):
        push(j)

    in_col.wait()
    col_low[...] = vcol[...].astype(BF16)
    for cp in in_small:
        cp.wait()
    gcb[...] = jnp.zeros_like(gcb)

    def weigh(x):
        logs = jnp.log(jnp.maximum(x, 1.0))
        weight = jnp.exp(WEIGHT_POWER * (logs - math.log(COUNT_SCALE)))
        return jnp.where(x >= 1.0, jnp.minimum(weight, 1.0), 0.0), logs

    def residues(rows, column_bias, load, out):
        count = rows.shape[0]
        rbc[0:count] = column_bias
        pred[0:count] = lax.dot_general(
            rows, col_low[...], (((1,), (1,)), ((), ())), preferred_element_type=F32
        )

        def body(s, carry):
            o = pl.multiple_of(s * SUB, SUB)
            weight, logs = load(o)
            bias = rbc[pl.ds(o, SUB)][:, 0:1]
            value = weight * (pred[pl.ds(o, SUB)] + bias + cbias[...] - logs)
            out[pl.ds(o, SUB)] = value.astype(BF16)
            total = value[:, 0:LANES]
            for k in range(1, cols // LANES):
                total = total + value[:, k * LANES:(k + 1) * LANES]
            rbc[pl.ds(o, SUB)] = total
            down = value[0:8]
            for k in range(1, SUB // 8):
                down = down + value[k * 8:(k + 1) * 8]
            gcb[...] += down
            return carry

        lax.fori_loop(0, count // SUB, body, 0, unroll=UNROLL)

    def col_grads(low, rows):
        return lax.dot_general(
            low, rows, (((0,), (0,)), ((), ())), preferred_element_type=F32
        )

    def half_tile(which):
        def load(o):
            return weigh(c0[which, pl.ds(o, SUB)].astype(F32))

        residues(rows0[which], to_column(rb0[which]), load, res.at[which])
        gob[which] = to_line(rbc[...])
        gro[which] = jnp.dot(res[which], col_low[...], preferred_element_type=F32)

    def ready(j):
        send_counts[j].wait()

        def body(s, carry):
            at = pl.ds(pl.multiple_of(s * SUB, SUB), SUB)
            weight, logs = weigh(rcv[j, at].astype(F32))
            wgt[j, at] = weight
            lgs[j, at] = logs
            return carry

        lax.fori_loop(0, 2 * part // SUB, body, 0, unroll=UNROLL)

    swap_rows.wait()
    swap_rb.wait()
    in_c0.wait()
    half_tile(other)
    swap_gr = remote(gro.at[other], gin, ssem.at[2], rsem.at[2], col=other)
    swap_gr.start()
    swap_gb = remote(gob.at[other], gib, ssem.at[3], rsem.at[3], col=other)
    swap_gb.start()
    half_tile(mine)
    in_rmom.wait()
    swap_gr.wait()
    swap_gb.wait()
    value, moment = step(vrow[...], vrmom[...], gro[mine] + gin[...])
    vrow[...] = value
    vrmom[...] = moment
    rsend[...] = value.astype(BF16)
    value, moment = step(rb0[mine], rbm[...], gob[mine] + gib[...])
    rbsend[...] = value
    rbm[...] = moment
    go_rows = remote(rsend, rows1.at[mine], ssem.at[4], rsem.at[4], row=right)
    go_rows.start()
    go_rb = remote(rbsend, rb1.at[mine], ssem.at[5], rsem.at[5], row=right)
    go_rb.start()
    for j in range(EARLY, CHUNKS):
        push(j)

    def col_step(out):
        def body(s, carry):
            at = pl.ds(pl.multiple_of(s * 64, 64), 64)
            value, moment = step(vcol[at], vcmom[at], gc[at])
            out[at] = value
            if out is vcol:
                vcmom[at] = moment
                col_low[at] = value.astype(BF16)
            return carry

        lax.fori_loop(0, cols // 64, body, 0)
        grad = jnp.sum(gcb[...], axis=0, keepdims=True)
        value, moment = step(cbias[...], cbm[...], grad)
        return value, moment

    gc[...] = col_grads(
        res[...].reshape(2 * half, cols), rows0[...].reshape(2 * half, rows0.shape[2])
    )
    in_cmom.wait()
    value, moment = col_step(vcol)
    cbias[...] = value
    cbm[...] = moment
    gcb[...] = jnp.zeros_like(gcb)

    for j in range(BEFORE):
        ready(j)

    go_rows.wait()
    pass_rows = remote(rows1.at[mine], rows1.at[mine], ssem.at[6], rsem.at[6], col=other)
    pass_rows.start()
    go_rb.wait()
    pass_rb = remote(rb1.at[mine], rb1.at[mine], ssem.at[7], rsem.at[7], col=other)
    pass_rb.start()
    pass_rows.wait()
    pass_rb.wait()

    swaps = [
        remote(xs.at[j, other], xr.at[j], xsem.at[j], ysem.at[j], col=other)
        for j in range(CHUNKS)
    ]
    backs = [
        remote(bs.at[j], br.at[j], bsem.at[j], dsem.at[j], row=left)
        for j in range(CHUNKS)
    ]

    def give_back(j):
        swaps[j].wait()
        bs[j] = (xs[j, mine] + xr[j]).astype(BF16)
        backs[j].start()

    def add_col_grads(j, low, rows):
        grad = col_grads(low[...], rows)
        gc[...] = grad if j == 0 else gc[...] + grad

    rbcol = [to_column(rb1[s]) for s in (0, 1)]
    for j in range(CHUNKS):
        if j >= BEFORE:
            ready(j)
        at = slice(j * part, (j + 1) * part)

        def load(o):
            return wgt[j, pl.ds(o, SUB)], lgs[j, pl.ds(o, SUB)]

        rows = jnp.concatenate([rows1[0, at], rows1[1, at]], axis=0)
        bias = jnp.concatenate([rbcol[0][at], rbcol[1][at]], axis=0)
        low = res.at[j % 2, 0:2 * part]
        residues(rows, bias, load, low)
        grad = jnp.dot(low[...], col_low[...], preferred_element_type=F32)
        for s in (0, 1):
            xs[j, s] = grad[s * part:(s + 1) * part]
            bacc[s, at] = rbc[s * part:(s + 1) * part]
        swaps[j].start()
        if j > 0:
            give_back(j - 1)
        if j < CHUNKS - 1:
            add_col_grads(j, low, rows)

    for s in (0, 1):
        xsb[s] = to_line(bacc[s])
    swap_b = remote(xsb.at[other], xrb, ssem.at[8], rsem.at[8], col=other)
    swap_b.start()
    give_back(CHUNKS - 1)
    swap_b.wait()
    bsb[...] = xsb[mine] + xrb[...]
    back_b = remote(bsb, brb, ssem.at[9], rsem.at[9], row=left)
    back_b.start()

    add_col_grads(CHUNKS - 1, low, rows)
    value, moment = col_step(col_out)
    col_bias_out[...] = value

    for j in range(CHUNKS):
        backs[j].wait()
        at = slice(j * part, (j + 1) * part)
        value, moment = step(vrow[at], vrmom[at], br[j].astype(F32))
        row_out[at] = value
    back_b.wait()
    value, moment = step(rbsend[...], rbm[...], brb[...])
    row_bias_out[...] = value


def leave(*refs):
    sem = refs[-1]
    count = len(refs) // 2
    copies = [
        pltpu.make_async_copy(refs[k], refs[count + k], sem.at[k]) for k in range(count)
    ]
    for cp in copies:
        cp.start()
    for cp in copies:
        cp.wait()


def per_device(
    ring,
    counts,
    row_factors,
    row_moments,
    row_bias,
    row_bias_moments,
    col_factors,
    col_moments,
    col_bias,
    col_bias_moments,
):
    rounds, height, cols = counts.shape
    half, rank = row_factors.shape
    part = half // CHUNKS
    hbm = pl.BlockSpec(memory_space=pltpu.HBM)
    vmem = pl.BlockSpec(memory_space=pltpu.VMEM)
    dma = pltpu.SemaphoreType.DMA
    scratch = [
        pltpu.VMEM((2, half, cols), jnp.int32),
        pltpu.VMEM((CHUNKS, 2, part, cols), jnp.int32),
        pltpu.VMEM((half, rank), F32),
        pltpu.VMEM((half, rank), F32),
        pltpu.VMEM((cols, rank), F32),
        pltpu.VMEM((cols, rank), F32),
        pltpu.VMEM((cols, rank), BF16),
        pltpu.VMEM((2, half, rank), BF16),
        pltpu.VMEM((2, 1, half), F32),
        pltpu.VMEM((2, half, rank), BF16),
        pltpu.VMEM((2, 1, half), F32),
        pltpu.VMEM((half, rank), BF16),
        pltpu.VMEM((1, half), F32),
        pltpu.VMEM((CHUNKS, 2 * part, cols), BF16),
        pltpu.VMEM((CHUNKS, 2 * part, cols), BF16),
        pltpu.VMEM((half, cols), F32),
        pltpu.VMEM((2, half, cols), BF16),
        pltpu.VMEM((half, LANES), F32),
        pltpu.VMEM((2, half, LANES), F32),
        pltpu.VMEM((2, half, rank), F32),
        pltpu.VMEM((half, rank), F32),
        pltpu.VMEM((2, 1, half), F32),
        pltpu.VMEM((1, half), F32),
        pltpu.VMEM((cols, rank), F32),
        pltpu.VMEM((8, cols), F32),
        pltpu.VMEM((1, half), F32),
        pltpu.VMEM((1, cols), F32),
        pltpu.VMEM((1, cols), F32),
        pltpu.VMEM((CHUNKS, 2 * part, cols), F32),
        pltpu.VMEM((CHUNKS, 2 * part, cols), F32),
        pltpu.VMEM((CHUNKS, 2, part, rank), F32),
        pltpu.VMEM((CHUNKS, part, rank), F32),
        pltpu.VMEM((CHUNKS, part, rank), BF16),
        pltpu.VMEM((CHUNKS, part, rank), BF16),
        pltpu.VMEM((2, 1, half), F32),
        pltpu.VMEM((1, half), F32),
        pltpu.VMEM((1, half), F32),
        pltpu.VMEM((1, half), F32),
        dma((9 + CHUNKS,)),
        dma((10,)),
        dma((10,)),
        dma((CHUNKS,)),
        dma((CHUNKS,)),
        dma((CHUNKS,)),
        dma((CHUNKS,)),
        dma((CHUNKS,)),
        dma((CHUNKS,)),
    ]
    shapes = ((half, rank), (1, half), (cols, rank), (1, cols))
    found = pl.pallas_call(
        functools.partial(kernel, ring),
        out_shape=[pltpu.VMEM(shape, F32) for shape in shapes],
        in_specs=[hbm] * 9,
        out_specs=[vmem] * 4,
        scratch_shapes=scratch,
        compiler_params=pltpu.CompilerParams(
            collective_id=0, has_side_effects=True, vmem_limit_bytes=56 * 1024 * 1024
        ),
    )(
        counts.reshape(rounds, 2, half, cols),
        row_factors,
        row_moments,
        row_bias.reshape(1, half),
        row_bias_moments.reshape(1, half),
        col_factors,
        col_moments,
        col_bias.reshape(1, cols),
        col_bias_moments.reshape(1, cols),
    )
    row_new, row_level, col_new, col_level = pl.pallas_call(
        leave,
        out_shape=[jax.ShapeDtypeStruct(shape, F32) for shape in shapes],
        in_specs=[vmem] * 4,
        out_specs=[hbm] * 4,
        scratch_shapes=[dma((4,))],
        compiler_params=pltpu.CompilerParams(vmem_limit_bytes=2 * 1024 * 1024),
    )(*found)
    return row_new, row_level.reshape(half), col_new, col_level.reshape(cols)


def solution(mesh):
    in_specs = (
        P(None, ("groups", "row"), "col"),
        P(("groups", "row", "col"), None),
        P(("groups", "row", "col"), None),
        P(("groups", "row", "col")),
        P(("groups", "row", "col")),
        P(("groups", "row", "col"), None),
        P(("groups", "row", "col"), None),
        P(("groups", "row", "col")),
        P(("groups", "row", "col")),
    )
    out_specs = (
        P(("groups", "row", "col"), None),
        P(("groups", "row", "col")),
        P(("groups", "row", "col"), None),
        P(("groups", "row", "col")),
    )
    return jax.shard_map(
        functools.partial(per_device, mesh.shape["row"]),
        mesh=mesh, in_specs=in_specs, out_specs=out_specs, check_vma=False,
    )
```

```python
import functools
import math

import jax
import jax.numpy as jnp
from jax import lax
from jax.experimental import pallas as pl
from jax.experimental.pallas import tpu as pltpu
from jax.sharding import PartitionSpec as P


LEARN_RATE = 0.25
COUNT_SCALE = 100.0
WEIGHT_POWER = 0.75
CHUNKS = 4
EARLY = 3
SUB = 16
UNROLL = 4
BEFORE = 3
LANES = 128
MESH = pl.DeviceIdType.MESH
F32 = jnp.float32
BF16 = jnp.bfloat16


def step(value, moment, grad):
    moment = moment + grad * grad
    return value - LEARN_RATE * grad * lax.rsqrt(moment), moment


def to_column(line):
    return jnp.transpose(jnp.broadcast_to(line, (LANES, line.shape[1])))


def to_line(column):
    return jnp.sum(jnp.transpose(column), axis=0, keepdims=True)


def kernel(
    ring,
    counts, row_factors, row_moments, row_bias, row_bias_mom,
    col_factors, col_moments, col_bias, col_bias_mom,
    row_out, row_bias_out, col_out, col_bias_out,
    c0, c1, vrow, vrmom, vcol, vcmom, col_low,
    rows0, rb0, rows1, rb1, rsend, rbsend, snd, rcv,
    pred, res, rbc, bacc, gro, gin, gob, gib, gc, gcb,
    rbm, cbias, cbm, wgt, lgs,
    xs, xr, bs, br, xsb, xrb, bsb, brb,
    lsem, ssem, rsem, csem, ksem, xsem, ysem,
    bsem, dsem,
):
    me = lax.axis_index("row")
    mine = lax.axis_index("col")
    other = 1 - mine
    right = lax.rem(me + 1, ring)
    left = lax.rem(me + ring - 1, ring)
    half = vrow.shape[0]
    part = half // CHUNKS
    cols = vcol.shape[0]

    def local(src, dst, k):
        cp = pltpu.make_async_copy(src, dst, lsem.at[k])
        cp.start()
        return cp

    def remote(src, dst, s, r, **where):
        return pltpu.make_async_remote_copy(
            src_ref=src, dst_ref=dst, send_sem=s, recv_sem=r,
            device_id=where, device_id_type=MESH,
        )

    in_row = local(row_factors, vrow, 0)
    in_rb = local(row_bias, rb0.at[mine], 5 + CHUNKS)
    in_c1 = [
        local(counts.at[1, :, pl.ds(j * part, part), :], c1.at[j], 1 + j)
        for j in range(CHUNKS)
    ]
    in_col = local(col_factors, vcol, 1 + CHUNKS)
    in_c0 = local(counts.at[0], c0, 2 + CHUNKS)
    in_rmom = local(row_moments, vrmom, 3 + CHUNKS)
    in_cmom = local(col_moments, vcmom, 4 + CHUNKS)

    in_small = [
        local(row_bias_mom, rbm, 6 + CHUNKS),
        local(col_bias, cbias, 7 + CHUNKS),
        local(col_bias_mom, cbm, 8 + CHUNKS),
    ]

    barrier = pltpu.get_barrier_semaphore()
    pl.semaphore_signal(barrier, inc=1, device_id={"row": left}, device_id_type=MESH)
    pl.semaphore_signal(barrier, inc=1, device_id={"row": right}, device_id_type=MESH)
    pl.semaphore_signal(barrier, inc=1, device_id={"col": other}, device_id_type=MESH)

    in_row.wait()
    rows0[mine] = vrow[...].astype(BF16)
    in_rb.wait()
    pl.semaphore_wait(barrier, 3)
    swap_rows = remote(rows0.at[mine], rows0.at[mine], ssem.at[0], rsem.at[0], col=other)
    swap_rows.start()
    swap_rb = remote(rb0.at[mine], rb0.at[mine], ssem.at[1], rsem.at[1], col=other)
    swap_rb.start()

    send_counts = [
        remote(snd.at[j], rcv.at[j], csem.at[j], ksem.at[j], row=right)
        for j in range(CHUNKS)
    ]

    def push(j):
        in_c1[j].wait()
        for s in (0, 1):
            snd[j, pl.ds(s * part, part)] = c1[j, s].astype(F32).astype(BF16)
        send_counts[j].start()

    for j in range(EARLY):
        push(j)

    in_col.wait()
    col_low[...] = vcol[...].astype(BF16)
    for cp in in_small:
        cp.wait()
    gcb[...] = jnp.zeros_like(gcb)

    def weigh(x):
        logs = jnp.log(jnp.maximum(x, 1.0))
        weight = jnp.exp(WEIGHT_POWER * (logs - math.log(COUNT_SCALE)))
        return jnp.where(x >= 1.0, jnp.minimum(weight, 1.0), 0.0), logs

    def residues(rows, column_bias, load, out):
        count = rows.shape[0]
        rbc[0:count] = column_bias
        pred[0:count] = lax.dot_general(
            rows, col_low[...], (((1,), (1,)), ((), ())), preferred_element_type=F32
        )

        def body(s, carry):
            o = pl.multiple_of(s * SUB, SUB)
            weight, logs = load(o)
            bias = rbc[pl.ds(o, SUB)][:, 0:1]
            value = weight * (pred[pl.ds(o, SUB)] + bias + cbias[...] - logs)
            out[pl.ds(o, SUB)] = value.astype(BF16)
            total = value[:, 0:LANES]
            for k in range(1, cols // LANES):
                total = total + value[:, k * LANES:(k + 1) * LANES]
            rbc[pl.ds(o, SUB)] = total
            down = value[0:8]
            for k in range(1, SUB // 8):
                down = down + value[k * 8:(k + 1) * 8]
            gcb[...] += down
            return carry

        lax.fori_loop(0, count // SUB, body, 0, unroll=UNROLL)

    def col_grads(low, rows):
        return lax.dot_general(
            low, rows, (((0,), (0,)), ((), ())), preferred_element_type=F32
        )

    def half_tile(which):
        def load(o):
            return weigh(c0[which, pl.ds(o, SUB)].astype(F32))

        residues(rows0[which], to_column(rb0[which]), load, res.at[which])
        gob[which] = to_line(rbc[...])
        gro[which] = jnp.dot(res[which], col_low[...], preferred_element_type=F32)

    def ready(j):
        send_counts[j].wait()

        def body(s, carry):
            at = pl.ds(pl.multiple_of(s * SUB, SUB), SUB)
            weight, logs = weigh(rcv[j, at].astype(F32))
            wgt[j, at] = weight
            lgs[j, at] = logs
            return carry

        lax.fori_loop(0, 2 * part // SUB, body, 0, unroll=UNROLL)

    swap_rows.wait()
    swap_rb.wait()
    in_c0.wait()
    half_tile(other)
    swap_gr = remote(gro.at[other], gin, ssem.at[2], rsem.at[2], col=other)
    swap_gr.start()
    swap_gb = remote(gob.at[other], gib, ssem.at[3], rsem.at[3], col=other)
    swap_gb.start()
    half_tile(mine)
    in_rmom.wait()
    swap_gr.wait()
    swap_gb.wait()
    value, moment = step(vrow[...], vrmom[...], gro[mine] + gin[...])
    vrow[...] = value
    vrmom[...] = moment
    rsend[...] = value.astype(BF16)
    value, moment = step(rb0[mine], rbm[...], gob[mine] + gib[...])
    rbsend[...] = value
    rbm[...] = moment
    go_rows = remote(rsend, rows1.at[mine], ssem.at[4], rsem.at[4], row=right)
    go_rows.start()
    go_rb = remote(rbsend, rb1.at[mine], ssem.at[5], rsem.at[5], row=right)
    go_rb.start()
    for j in range(EARLY, CHUNKS):
        push(j)

    def col_step(out):
        def body(s, carry):
            at = pl.ds(pl.multiple_of(s * 64, 64), 64)
            value, moment = step(vcol[at], vcmom[at], gc[at])
            out[at] = value
            if out is vcol:
                vcmom[at] = moment
                col_low[at] = value.astype(BF16)
            return carry

        lax.fori_loop(0, cols // 64, body, 0)
        grad = jnp.sum(gcb[...], axis=0, keepdims=True)
        value, moment = step(cbias[...], cbm[...], grad)
        return value, moment

    gc[...] = col_grads(
        res[...].reshape(2 * half, cols), rows0[...].reshape(2 * half, rows0.shape[2])
    )
    in_cmom.wait()
    value, moment = col_step(vcol)
    cbias[...] = value
    cbm[...] = moment
    gcb[...] = jnp.zeros_like(gcb)

    for j in range(BEFORE):
        ready(j)

    go_rows.wait()
    pass_rows = remote(rows1.at[mine], rows1.at[mine], ssem.at[6], rsem.at[6], col=other)
    pass_rows.start()
    go_rb.wait()
    pass_rb = remote(rb1.at[mine], rb1.at[mine], ssem.at[7], rsem.at[7], col=other)
    pass_rb.start()
    pass_rows.wait()
    pass_rb.wait()

    swaps = [
        remote(xs.at[j, other], xr.at[j], xsem.at[j], ysem.at[j], col=other)
        for j in range(CHUNKS)
    ]
    backs = [
        remote(bs.at[j], br.at[j], bsem.at[j], dsem.at[j], row=left)
        for j in range(CHUNKS)
    ]

    def give_back(j):
        swaps[j].wait()
        bs[j] = (xs[j, mine] + xr[j]).astype(BF16)
        backs[j].start()

    def add_col_grads(j, low, rows):
        grad = col_grads(low[...], rows)
        gc[...] = grad if j == 0 else gc[...] + grad

    rbcol = [to_column(rb1[s]) for s in (0, 1)]
    for j in range(CHUNKS):
        if j >= BEFORE:
            ready(j)
        at = slice(j * part, (j + 1) * part)

        def load(o):
            return wgt[j, pl.ds(o, SUB)], lgs[j, pl.ds(o, SUB)]

        rows = jnp.concatenate([rows1[0, at], rows1[1, at]], axis=0)
        bias = jnp.concatenate([rbcol[0][at], rbcol[1][at]], axis=0)
        low = res.at[j % 2, 0:2 * part]
        residues(rows, bias, load, low)
        grad = jnp.dot(low[...], col_low[...], preferred_element_type=F32)
        for s in (0, 1):
            xs[j, s] = grad[s * part:(s + 1) * part]
            bacc[s, at] = rbc[s * part:(s + 1) * part]
        swaps[j].start()
        if j > 0:
            give_back(j - 1)
        if j < CHUNKS - 1:
            add_col_grads(j, low, rows)

    for s in (0, 1):
        xsb[s] = to_line(bacc[s])
    swap_b = remote(xsb.at[other], xrb, ssem.at[8], rsem.at[8], col=other)
    swap_b.start()
    give_back(CHUNKS - 1)
    swap_b.wait()
    bsb[...] = xsb[mine] + xrb[...]
    back_b = remote(bsb, brb, ssem.at[9], rsem.at[9], row=left)
    back_b.start()

    add_col_grads(CHUNKS - 1, low, rows)
    value, moment = col_step(col_out)
    col_bias_out[...] = value

    for j in range(CHUNKS):
        backs[j].wait()
        at = slice(j * part, (j + 1) * part)
        value, moment = step(vrow[at], vrmom[at], br[j].astype(F32))
        row_out[at] = value
    back_b.wait()
    value, moment = step(rbsend[...], rbm[...], brb[...])
    row_bias_out[...] = value


def leave(*refs):
    sem = refs[-1]
    count = len(refs) // 2
    copies = [
        pltpu.make_async_copy(refs[k], refs[count + k], sem.at[k]) for k in range(count)
    ]
    for cp in copies:
        cp.start()
    for cp in copies:
        cp.wait()


def per_device(
    ring,
    counts,
    row_factors,
    row_moments,
    row_bias,
    row_bias_moments,
    col_factors,
    col_moments,
    col_bias,
    col_bias_moments,
):
    rounds, height, cols = counts.shape
    half, rank = row_factors.shape
    part = half // CHUNKS
    hbm = pl.BlockSpec(memory_space=pltpu.HBM)
    vmem = pl.BlockSpec(memory_space=pltpu.VMEM)
    dma = pltpu.SemaphoreType.DMA
    scratch = [
        pltpu.VMEM((2, half, cols), jnp.int32),
        pltpu.VMEM((CHUNKS, 2, part, cols), jnp.int32),
        pltpu.VMEM((half, rank), F32),
        pltpu.VMEM((half, rank), F32),
        pltpu.VMEM((cols, rank), F32),
        pltpu.VMEM((cols, rank), F32),
        pltpu.VMEM((cols, rank), BF16),
        pltpu.VMEM((2, half, rank), BF16),
        pltpu.VMEM((2, 1, half), F32),
        pltpu.VMEM((2, half, rank), BF16),
        pltpu.VMEM((2, 1, half), F32),
        pltpu.VMEM((half, rank), BF16),
        pltpu.VMEM((1, half), F32),
        pltpu.VMEM((CHUNKS, 2 * part, cols), BF16),
        pltpu.VMEM((CHUNKS, 2 * part, cols), BF16),
        pltpu.VMEM((half, cols), F32),
        pltpu.VMEM((2, half, cols), BF16),
        pltpu.VMEM((half, LANES), F32),
        pltpu.VMEM((2, half, LANES), F32),
        pltpu.VMEM((2, half, rank), F32),
        pltpu.VMEM((half, rank), F32),
        pltpu.VMEM((2, 1, half), F32),
        pltpu.VMEM((1, half), F32),
        pltpu.VMEM((cols, rank), F32),
        pltpu.VMEM((8, cols), F32),
        pltpu.VMEM((1, half), F32),
        pltpu.VMEM((1, cols), F32),
        pltpu.VMEM((1, cols), F32),
        pltpu.VMEM((CHUNKS, 2 * part, cols), F32),
        pltpu.VMEM((CHUNKS, 2 * part, cols), F32),
        pltpu.VMEM((CHUNKS, 2, part, rank), F32),
        pltpu.VMEM((CHUNKS, part, rank), F32),
        pltpu.VMEM((CHUNKS, part, rank), BF16),
        pltpu.VMEM((CHUNKS, part, rank), BF16),
        pltpu.VMEM((2, 1, half), F32),
        pltpu.VMEM((1, half), F32),
        pltpu.VMEM((1, half), F32),
        pltpu.VMEM((1, half), F32),
        dma((9 + CHUNKS,)),
        dma((10,)),
        dma((10,)),
        dma((CHUNKS,)),
        dma((CHUNKS,)),
        dma((CHUNKS,)),
        dma((CHUNKS,)),
        dma((CHUNKS,)),
        dma((CHUNKS,)),
    ]
    shapes = ((half, rank), (1, half), (cols, rank), (1, cols))
    found = pl.pallas_call(
        functools.partial(kernel, ring),
        out_shape=[pltpu.VMEM(shape, F32) for shape in shapes],
        in_specs=[hbm] * 9,
        out_specs=[vmem] * 4,
        scratch_shapes=scratch,
        compiler_params=pltpu.CompilerParams(
            collective_id=0, has_side_effects=True, vmem_limit_bytes=56 * 1024 * 1024
        ),
    )(
        counts.reshape(rounds, 2, half, cols),
        row_factors,
        row_moments,
        row_bias.reshape(1, half),
        row_bias_moments.reshape(1, half),
        col_factors,
        col_moments,
        col_bias.reshape(1, cols),
        col_bias_moments.reshape(1, cols),
    )
    row_new, row_level, col_new, col_level = pl.pallas_call(
        leave,
        out_shape=[jax.ShapeDtypeStruct(shape, F32) for shape in shapes],
        in_specs=[vmem] * 4,
        out_specs=[hbm] * 4,
        scratch_shapes=[dma((4,))],
        compiler_params=pltpu.CompilerParams(vmem_limit_bytes=2 * 1024 * 1024),
    )(*found)
    return row_new, row_level.reshape(half), col_new, col_level.reshape(cols)


def solution(mesh):
    in_specs = (
        P(None, ("groups", "row"), "col"),
        P(("groups", "row", "col"), None),
        P(("groups", "row", "col"), None),
        P(("groups", "row", "col")),
        P(("groups", "row", "col")),
        P(("groups", "row", "col"), None),
        P(("groups", "row", "col"), None),
        P(("groups", "row", "col")),
        P(("groups", "row", "col")),
    )
    out_specs = (
        P(("groups", "row", "col"), None),
        P(("groups", "row", "col")),
        P(("groups", "row", "col"), None),
        P(("groups", "row", "col")),
    )
    return jax.shard_map(
        functools.partial(per_device, mesh.shape["row"]),
        mesh=mesh, in_specs=in_specs, out_specs=out_specs, check_vma=False,
    )
```
